32 devices in a mesh: shard: 8 (over z, y), dp: 4 (over x, core).
Axes of the slice: x: 2, y: 2, z: 4, core: 2. Of those that a mesh axis runs over, the one named last changes fastest.
Arguments:
- cold_table: bfloat16 [16384, 256], P('shard'), may hold values from -6 to 6
- cold_accum: float32 [16384], P('shard'), may hold values from 0.005 to 0.5
- dither_bits: int32 [16384, 256], P('shard'), may hold values from 0 to 65280
- hot_table: float32 [1024, 256], replicated, may hold values from -6 to 6
- hot_accum: float32 [1024], replicated, may hold values from 1 to 100
- w_flat: bfloat16 [4096, 512], replicated, may hold values from -0.09375 to 0.09375
- w_inter: bfloat16 [256, 512], replicated, may hold values from -0.09375 to 0.09375
- hidden_bias: float32 [512], replicated, may hold values from -1 to 1
- w_out: float32 [512], replicated, may hold values from -0.25 to 0.25
- targets: float32 [16384], P(('shard', 'dp')), may hold values from 0 to 1
- hot_ids: int32 [16384, 8], P(('shard', 'dp')), may hold values from 0 to 1023
- cold_slots: int32 [16384, 8], P(('shard', 'dp')), may hold values from 0 to 2047, as said below
- requests: int32 [512, 256], P(('shard', 'dp')), may hold values from 0 to 2047, as said below
- counts: int32 [64, 8], P(('shard', 'dp')), may hold values from 1 to 256, as said below
Outputs:
- cold_out: bfloat16 [16384, 256], P('shard')
- cold_accum_out: float32 [16384], P('shard')
- hot_out: float32 [1024, 256], replicated
- hot_accum_out: float32 [1024], replicated
The draws below stay inside these ranges and needn't reach their ends.
Inputs may be any that keep to these rules, and one draw needn't show every extreme that they name: `requests`: in each row of 256 entries (one device, micro-batch and shard) the entries name distinct rows of that shard's 2048; only the first counts-many are live, the rest name arbitrary rows. `counts`: in every draw, each device has in each micro-batch a shard with exactly 256 live slots. `cold_slots`: index into its device's request rows of that micro-batch, shard * 256 + slot; always a live slot, and every live slot is named by some lookup.
All inputs are finite; a program needn't handle non-finite values.
Results may differ from the reference program's by a relative error of at most 0.001.
The reference program's roundings to bfloat16 on the way (of `stacked`, `pair_dots`, `slopes` and `mirror`) count: a program that leaves them out, or rounds other values in their place, can miss the bound.
Values may be sent and summed in bfloat16 or wider, within the bound.
A program may use at most 128 MiB of HBM per device.

```python
import math
import jax
import jax.numpy as jnp
import numpy as np
from jax import lax

E = 256
HID = 512
F_COLD = 8
F_HOT = 8
MB = 2
HOT = 1024
BATCH = 256
ROWS_DEV = 2048
FEATS = 16
COLD_ROWS = 16384
SAMPLES = 16384
N_SHARD = 8
N_DP = 4


def request_plan(key):
    base = jax.random.fold_in(key, 4242)
    keys = jax.random.split(base, 6)
    capacity = BATCH * F_COLD // N_SHARD
    device_count = N_SHARD * N_DP
    lookups = BATCH * F_COLD
    levels = jax.random.randint(keys[0], (N_SHARD,), 1, 5)
    low_counts = jnp.maximum(levels * capacity // 8, 1)
    high_counts = jnp.maximum(levels * capacity // 4, low_counts) + 1
    counts = jax.random.randint(keys[1], (device_count, MB, N_SHARD), low_counts, high_counts)
    requester = jnp.arange(device_count)[:, None, None]
    micro_index = jnp.arange(MB)[None, :, None]
    owners = jnp.arange(N_SHARD)[None, None, :]
    counts = jnp.where(owners == (requester + micro_index) % N_SHARD, capacity, counts)
    row_orders = jax.vmap(lambda part_key: jax.random.permutation(part_key, ROWS_DEV))(jax.random.split(keys[2], N_SHARD))
    starts = jax.random.randint(keys[3], (device_count, MB, N_SHARD, 1), 0, ROWS_DEV)
    positions = (starts + jnp.arange(capacity)[None, None, None, :]) % ROWS_DEV
    requests = row_orders[jnp.arange(N_SHARD)[None, None, :, None], positions]
    live_total = jnp.sum(counts, axis=-1, keepdims=True)
    ends = jnp.cumsum(counts, axis=-1)
    order = jnp.arange(lookups)[None, None, :]
    random_pick = jax.random.randint(keys[4], (device_count, MB, lookups), 0, live_total)
    flat_index = jnp.where(order < live_total, order, random_pick)
    owner_of = jax.vmap(jax.vmap(lambda boundaries, chosen: jnp.searchsorted(boundaries, chosen, side='right')))(ends, flat_index)
    owner_of = owner_of.astype(jnp.int32)
    begins = ends - counts
    within = flat_index - jnp.take_along_axis(begins, owner_of, axis=-1)
    slot_index = owner_of * capacity + within
    shuffles = jax.vmap(lambda part_key: jax.random.permutation(part_key, lookups))(jax.random.split(keys[5], device_count * MB))
    slot_index = jnp.take_along_axis(slot_index, shuffles.reshape(device_count, MB, lookups), axis=-1)
    return (requests.reshape(device_count * MB * N_SHARD, capacity).astype(jnp.int32), counts.reshape(device_count * MB, N_SHARD).astype(jnp.int32), slot_index.reshape(device_count * MB * BATCH, F_COLD).astype(jnp.int32))


def draw_requests(key, part):
    return request_plan(key)[0]


def draw_counts(key, part):
    return request_plan(key)[1]


def draw_cold_slots(key, part):
    return request_plan(key)[2]


def with_ends(entries, stream_key, low, largest):
    shape = entries.shape
    index_at = [jax.random.randint(jax.random.fold_in(stream_key, axis), (), 0, shape[axis]) for axis in range(len(shape))]
    entries = entries.at[tuple(index_at)].set(low)
    longest = shape.index(max(shape))
    index_at[longest] = (index_at[longest] + 1) % shape[longest]
    return entries.at[tuple(index_at)].set(largest)


def steps_of(rng, shape, shards, smallest, largest):
    def one(dim, parts):
        draws = jax.random.uniform(jax.random.fold_in(jax.random.fold_in(rng, 6), dim), (parts,), jnp.float32, smallest / len(shards), largest / len(shards))
        return jnp.repeat(jnp.exp(draws), shape[dim] // parts).reshape((-1,) + (1,) * (len(shape) - dim - 1))

    factor_of = one(*shards[0])
    for cut in shards[1:]:
        factor_of = factor_of * one(*cut)
    return factor_of


def cumulative_ranks(count, slope):
    weights = [(1 << 20) // math.isqrt(grade ** slope) + 1 for grade in range(1, count + 1)]
    spread = 1 + sum(weights) // (1 << 30)
    return np.cumsum(np.array([max(1, weight // spread) for weight in weights]))


def skewed_ids(key, extent, number_of, lean):
    listing = cumulative_ranks(number_of, lean)
    pick = jax.random.randint(jax.random.fold_in(key, 1), extent, 0, int(listing[number_of - 1]))
    rank = jnp.searchsorted(jnp.asarray(listing, jnp.int32), pick, side="right")
    return jax.random.permutation(jax.random.fold_in(key, 2), number_of)[rank].astype(jnp.int32)


def gaussian(key, shape, deviation, most, cuts=(), kind=jnp.bfloat16):
    factor_of = steps_of(key, shape, cuts, -0.22, 0.18) if cuts else 1.0
    entries = jax.random.normal(key, shape, jnp.float32) * deviation * factor_of
    return jnp.minimum(jnp.maximum(entries, -most), most).astype(kind)


def setup_inputs(seed: int = 0) -> dict:
    key_list = jax.random.split(jax.random.key(seed), 15)
    return {
        "cold_table": gaussian(key_list[0], (COLD_ROWS, E), 1.0, 6.0, ((0, 8),)),
        "cold_accum": jnp.clip(jnp.exp(math.log(0.5) - 4.6051702 * jax.random.uniform(key_list[1], (COLD_ROWS,), jnp.float32) ** steps_of(key_list[1], (COLD_ROWS,), ((0, 8),), -0.2, 0.2)), 0.005, 0.5),
        "dither_bits": with_ends(jax.random.randint(key_list[2], (COLD_ROWS, E), 0, 65281), jax.random.fold_in(key_list[2], 1), 0, 65280).astype(jnp.int32),
        "hot_table": gaussian(key_list[3], (HOT, E), 1.0, 6.0, (), jnp.float32),
        "hot_accum": jnp.clip(jnp.exp(jax.random.uniform(key_list[4], (HOT,), jnp.float32, math.log(1.0), math.log(100.0))), 1.0, 100.0),
        "w_flat": gaussian(key_list[5], (FEATS * E, HID), (FEATS * E) ** -0.5, 0.09375),
        "w_inter": gaussian(key_list[6], (FEATS * FEATS, HID), (FEATS * E) ** -0.5, 0.09375),
        "hidden_bias": jnp.clip(jax.random.uniform(key_list[7], (HID,), jnp.float32, -1.0, 1.0), -1.0, 1.0),
        "w_out": gaussian(key_list[8], (HID,), HID ** -0.5, 0.25, (), jnp.float32),
        "targets": jnp.clip(1.0 * jax.random.uniform(key_list[9], (SAMPLES,), jnp.float32) ** steps_of(key_list[9], (SAMPLES,), ((0, 32),), -0.2, 0.2), 0.0, 1.0),
        "hot_ids": with_ends(skewed_ids(key_list[10], (SAMPLES, F_HOT), HOT, 2), jax.random.fold_in(key_list[10], 3), 0, HOT - 1).astype(jnp.int32),
        "cold_slots": draw_cold_slots(jax.random.fold_in(key_list[14], 71), 0),
        "requests": draw_requests(jax.random.fold_in(key_list[14], 71), 0),
        "counts": draw_counts(jax.random.fold_in(key_list[14], 71), 0),
    }


learn_rate = 0.3

def backprop(stacked, targets, w_flat, w_inter, hidden_bias, w_out):
    row_count, feature_count, row_width = stacked.shape
    flattened = stacked.reshape(row_count, feature_count * row_width)
    widened = stacked.astype(jnp.float32)
    pair_dots = (jnp.einsum('sfe,sge->sfg', widened, widened) * row_width ** (-0.5)).astype(jnp.bfloat16)
    pre_act = jnp.dot(flattened, w_flat, preferred_element_type=jnp.float32)
    pre_act = pre_act + jnp.dot(pair_dots.reshape(row_count, feature_count * feature_count), w_inter, preferred_element_type=jnp.float32)
    pre_act = pre_act + hidden_bias
    gated = jax.nn.sigmoid(pre_act)
    logits = lax.optimization_barrier(jnp.sum(pre_act * gated * w_out, axis=-1))
    residual = jax.nn.sigmoid(logits) - targets
    slopes = (residual[:, None] * w_out * gated * (1.0 + pre_act * (1.0 - gated))).astype(jnp.bfloat16)
    back_flat = jnp.dot(slopes, w_flat.T, preferred_element_type=jnp.float32)
    back_pairs = jnp.dot(slopes, w_inter.T, preferred_element_type=jnp.float32).reshape(row_count, feature_count, feature_count)
    mirror = ((back_pairs + jnp.swapaxes(back_pairs, 1, 2)) * row_width ** (-0.5)).astype(jnp.bfloat16)
    return back_flat.reshape(row_count, feature_count, row_width) + jnp.einsum('sfg,sge->sfe', mirror.astype(jnp.float32), widened)

def adagrad_rows(table_rows, accum, gradient):
    accum_new = accum + lax.optimization_barrier(jnp.mean(gradient * gradient, axis=-1))
    updated = table_rows - learn_rate * gradient / jnp.sqrt(accum_new)[:, None]
    return (updated, accum_new)

def requantize(updated, bits, touched):
    grid_step = lax.optimization_barrier(jnp.max(jnp.abs(updated), axis=-1, keepdims=True)) / 8.0
    dither = bits.astype(jnp.float32) * (1.0 / 65280.0) - 0.5
    return jnp.where(touched[:, None], updated + grid_step * dither, updated).astype(jnp.bfloat16)

def reference(cold_table, cold_accum, dither_bits, hot_table, hot_accum, w_flat, w_inter, hidden_bias, w_out, targets, hot_ids, cold_slots, requests, counts):
    device_count = N_SHARD * N_DP
    capacity = requests.shape[1]
    per_device = MB * BATCH
    request_rows = requests.reshape(device_count, MB, N_SHARD, capacity)
    slot_rows = cold_slots.reshape(device_count, per_device, F_COLD)
    hot_rows = hot_ids.reshape(device_count, per_device, F_HOT)
    target_rows = targets.reshape(device_count, per_device)
    micro_index = (jnp.arange(per_device, dtype=jnp.int32) // BATCH)[:, None]

    def visit(totals, per_dev):
        hot_grad, cold_grad = totals
        dev_requests, dev_slots, dev_hot, dev_targets = per_dev
        owners = dev_slots // capacity
        slot_index = dev_slots % capacity
        local_rows = dev_requests[micro_index, owners, slot_index]
        row_id = owners * ROWS_DEV + local_rows
        stacked = jnp.concatenate([cold_table[row_id], hot_table[dev_hot].astype(jnp.bfloat16)], axis=1)
        gradients = backprop(stacked, dev_targets, w_flat, w_inter, hidden_bias, w_out)
        hot_grad = hot_grad + jax.ops.segment_sum(gradients[:, F_COLD:].reshape(-1, E), dev_hot.reshape(-1), num_segments=HOT)
        cold_grad = cold_grad.at[row_id.reshape(-1)].add(gradients[:, :F_COLD].reshape(-1, E))
        return ((hot_grad, cold_grad), None)
    start = (jnp.zeros((HOT, E), jnp.float32), jnp.zeros((COLD_ROWS, E), jnp.float32))
    (hot_grad, cold_grad), _ = lax.scan(visit, start, (request_rows, slot_rows, hot_rows, target_rows))
    live_mask = (jnp.arange(capacity, dtype=jnp.int32)[None, None, None, :] < counts.reshape(device_count, MB, N_SHARD)[..., None]).astype(jnp.float32)
    owner_grid = jnp.arange(N_SHARD, dtype=jnp.int32)[None, None, :, None]
    global_rows = owner_grid * ROWS_DEV + request_rows
    touched = jnp.zeros((COLD_ROWS,), jnp.float32).at[global_rows.reshape(-1)].add(live_mask.reshape(-1))
    averaged = cold_grad / jnp.maximum(touched, 1.0)[:, None]
    updated, cold_accum_out = adagrad_rows(cold_table.astype(jnp.float32), cold_accum, averaged)
    cold_out = requantize(updated, dither_bits, touched > 0.5)
    hot_out, hot_accum_out = adagrad_rows(hot_table, hot_accum, hot_grad)
    return (cold_out, cold_accum_out, hot_out, hot_accum_out)
```

```python
import functools

import jax
import jax.numpy as jnp
from jax import lax
from jax.experimental import pallas as pl
from jax.experimental.pallas import tpu as pltpu
from jax.sharding import PartitionSpec as P

learn_rate = 0.3
BF = jnp.bfloat16
F32 = jnp.float32
VMEM_LIMIT = 52 * 1024 * 1024


def dot(a, b):
    return lax.dot_general(a, b, (((1,), (0,)), ((), ())), preferred_element_type=F32)


def dot_t(a, b):
    return lax.dot_general(a, b, (((1,), (1,)), ((), ())), preferred_element_type=F32)


def hot_one(rows, columns, ids, axis, first):
    spots = lax.broadcasted_iota(jnp.int32, (rows, columns), axis) + first
    return jnp.where(spots == ids, 1.0, 0.0)


def owner_gather_kernel(ids_ref, table_ref, rows_ref, hits_ref):
    rows = table_ref.shape[0]
    pick = hot_one(ids_ref.shape[0], rows, ids_ref[...], 1, 0)
    rows_ref[...] = dot(pick.astype(BF), table_ref[...]).astype(BF)

    @pl.when(pl.program_id(0) == 0)
    def _():
        hits_ref[...] = jnp.zeros_like(hits_ref)

    hits_ref[...] += jnp.sum(pick, axis=0, keepdims=True)


def owner_gather(ids, table):
    count, (rows, width) = ids.shape[0], table.shape
    tile = min(256, count)
    return pl.pallas_call(
        owner_gather_kernel,
        grid=(count // tile,),
        in_specs=[
            pl.BlockSpec((tile, 1), lambda i: (i, 0)),
            pl.BlockSpec((rows, width), lambda i: (0, 0)),
        ],
        out_specs=[
            pl.BlockSpec((tile, width), lambda i: (i, 0)),
            pl.BlockSpec((1, rows), lambda i: (0, 0)),
        ],
        out_shape=[
            jax.ShapeDtypeStruct((count, width), BF),
            jax.ShapeDtypeStruct((1, rows), F32),
        ],
        compiler_params=pltpu.CompilerParams(vmem_limit_bytes=VMEM_LIMIT),
        cost_estimate=pl.CostEstimate(
            flops=2 * count * rows * width,
            bytes_accessed=2 * (count + rows) * width,
            transcendentals=0,
        ),
    )(ids, table)


def owner_scatter_kernel(ids_ref, grad_ref, out_ref):
    tile = out_ref.shape[0]
    count = ids_ref.shape[1]
    pick = hot_one(tile, count, ids_ref[...], 0, pl.program_id(0) * tile)
    out_ref[...] = dot(pick.astype(BF), grad_ref[...]).astype(out_ref.dtype)


def owner_scatter(ids, grads, rows):
    count, width = grads.shape
    tile = min(256, rows)
    return pl.pallas_call(
        owner_scatter_kernel,
        grid=(rows // tile,),
        in_specs=[
            pl.BlockSpec((1, count), lambda i: (0, 0)),
            pl.BlockSpec((count, width), lambda i: (0, 0)),
        ],
        out_specs=pl.BlockSpec((tile, width), lambda i: (i, 0)),
        out_shape=jax.ShapeDtypeStruct((rows, width), BF),
        compiler_params=pltpu.CompilerParams(vmem_limit_bytes=VMEM_LIMIT),
        cost_estimate=pl.CostEstimate(
            flops=2 * count * rows * width,
            bytes_accessed=2 * (count + rows) * width,
            transcendentals=0,
        ),
    )(ids, grads)


def train_kernel(
    fetched_ref,
    cold_col_ref,
    cold_row_ref,
    hot_col_ref,
    hot_row_ref,
    hot_ref,
    w_flat_ref,
    w_inter_ref,
    w_turned_ref,
    bias_ref,
    w_out_ref,
    targets_ref,
    hot_before_ref,
    slot_grad_ref,
    hot_grad_ref,
    x_ref,
    pairs_ref,
    grad_ref,
    high_ref,
    low_ref,
):
    feats, samples, width = x_ref.shape
    cold = cold_col_ref.shape[0] // samples
    slots = fetched_ref.shape[0]
    hot_count = hot_ref.shape[0]
    scale = width ** (-0.5)
    group = 16
    side = feats * group
    square = feats * feats

    def fill_cold(f, carry):
        ids = cold_col_ref[pl.ds(pl.multiple_of(f * samples, samples), samples), :]
        pick = hot_one(samples, slots, ids, 1, 0).astype(BF)
        x_ref[f] = dot(pick, fetched_ref[...]).astype(BF)
        return carry

    lax.fori_loop(0, cold, fill_cold, 0)

    def fill_hot(f, carry):
        ids = hot_col_ref[pl.ds(pl.multiple_of(f * samples, samples), samples), :]
        pick = hot_one(samples, hot_count, ids, 1, 0).astype(BF)
        x_ref[f + cold] = dot(pick, hot_ref[...]).astype(BF)
        return carry

    lax.fori_loop(0, feats - cold, fill_hot, 0)

    def grid_of(shape, axis):
        return lax.broadcasted_iota(jnp.int32, shape, axis)

    same_sample = grid_of((side, side), 0) % group == grid_of((side, side), 1) % group
    same_feature = grid_of((side, square), 0) // group == grid_of((side, square), 1) // feats
    spread = jnp.where(
        grid_of((side, square), 0) // group == grid_of((side, square), 1) % feats, 1.0, 0.0
    ).astype(BF)

    def pair_step(b, carry):
        at = pl.ds(pl.multiple_of(b * group, group), group)
        part = x_ref[:, at, :].reshape(side, width)
        grams = dot_t(part, part) * scale
        grams = jnp.where(same_sample, grams, 0.0).astype(BF)
        wide = jnp.where(same_feature, dot(grams, spread), 0.0)
        pairs_ref[at, :] = jnp.sum(wide.reshape(feats, group, square), axis=0).astype(BF)
        return carry

    lax.fori_loop(0, samples // group, pair_step, 0, unroll=2)

    pre = dot(pairs_ref[...], w_inter_ref[...]) + bias_ref[...]
    for f in range(feats):
        pre = pre + dot(x_ref[f], w_flat_ref[f * width : (f + 1) * width, :])
    gated = jax.nn.sigmoid(pre)
    w_out = w_out_ref[...]
    logits = jnp.sum(pre * gated * w_out, axis=-1, keepdims=True)
    residual = jax.nn.sigmoid(logits) - targets_ref[...]
    slopes = (residual * w_out * gated * (1.0 + pre * (1.0 - gated))).astype(BF)

    mirror = (dot_t(slopes, w_inter_ref[...]) + dot_t(slopes, w_turned_ref[...])) * scale
    pairs_ref[...] = mirror.astype(BF)

    def mirror_step(b, carry):
        at = pl.ds(pl.multiple_of(b * group, group), group)
        part = x_ref[:, at, :].reshape(side, width)
        one = pairs_ref[at, :].astype(F32)
        many = jnp.broadcast_to(one[None], (feats, group, square)).reshape(side, square)
        many = jnp.where(same_feature, many, 0.0).astype(BF)
        turned = jnp.where(same_sample, dot_t(many, spread), 0.0).astype(BF)
        grad_ref[:, at, :] = dot(turned, part).reshape(feats, group, width)
        return carry

    lax.fori_loop(0, samples // group, mirror_step, 0, unroll=2)

    for f in range(feats):
        back = dot_t(slopes, w_flat_ref[f * width : (f + 1) * width, :]) + grad_ref[f]
        high = back.astype(BF)
        high_ref[f * samples : (f + 1) * samples, :] = high
        if f >= cold:
            low_ref[(f - cold) * samples : (f - cold + 1) * samples, :] = (
                back - high.astype(F32)
            ).astype(BF)

    tile = 256
    edge = cold * samples

    def spill_cold(c, carry):
        first = pl.multiple_of(c * tile, tile)
        pick = hot_one(tile, edge, cold_row_ref[...], 0, first).astype(BF)
        slot_grad_ref[pl.ds(first, tile), :] = dot(pick, high_ref[:edge, :]).astype(BF)
        return carry

    lax.fori_loop(0, slots // tile, spill_cold, 0)

    def spill_hot(c, carry):
        first = pl.multiple_of(c * tile, tile)
        pick = hot_one(tile, hot_row_ref.shape[1], hot_row_ref[...], 0, first).astype(BF)
        total = dot(pick, high_ref[edge:, :]) + dot(pick, low_ref[...])
        at = pl.ds(first, tile)
        hot_grad_ref[at, :] = hot_before_ref[at, :] + total
        return carry

    lax.fori_loop(0, hot_count // tile, spill_hot, 0)


def train(*operands):
    fetched, cold_col, _, hot_col, _, hot_rows, w_flat = operands[:7]
    samples = operands[11].shape[0]
    slots, width = fetched.shape
    feats = (cold_col.shape[0] + hot_col.shape[0]) // samples
    hidden = w_flat.shape[1]
    return pl.pallas_call(
        train_kernel,
        in_specs=[pl.BlockSpec(memory_space=pltpu.VMEM)] * len(operands),
        out_specs=[pl.BlockSpec(memory_space=pltpu.VMEM)] * 2,
        out_shape=[
            jax.ShapeDtypeStruct((slots, width), BF),
            jax.ShapeDtypeStruct(hot_rows.shape, F32),
        ],
        scratch_shapes=[
            pltpu.VMEM((feats, samples, width), BF),
            pltpu.VMEM((samples, feats * feats), BF),
            pltpu.VMEM((feats, samples, width), F32),
            pltpu.VMEM((feats * samples, width), BF),
            pltpu.VMEM((hot_col.shape[0], width), BF),
        ],
        compiler_params=pltpu.CompilerParams(vmem_limit_bytes=VMEM_LIMIT),
        cost_estimate=pl.CostEstimate(
            flops=4 * samples * feats * width * (hidden + slots + hot_rows.shape[0]),
            bytes_accessed=12 * 1024 * 1024,
            transcendentals=samples * hidden,
        ),
    )(*operands)


def cold_update_kernel(parts_ref, hits_ref, table_ref, accum_ref, bits_ref, out_ref, accum_out_ref):
    grad = parts_ref[0].astype(F32)
    for d in range(1, parts_ref.shape[0]):
        grad = grad + parts_ref[d].astype(F32)
    hits = hits_ref[...]
    averaged = grad / jnp.maximum(hits, 1.0)
    accum = accum_ref[...] + jnp.mean(averaged * averaged, axis=-1, keepdims=True)
    updated = table_ref[...].astype(F32) - learn_rate * averaged / jnp.sqrt(accum)
    step = jnp.max(jnp.abs(updated), axis=-1, keepdims=True) / 8.0
    dither = bits_ref[...].astype(F32) * (1.0 / 65280.0) - 0.5
    out_ref[...] = jnp.where(hits > 0.5, updated + step * dither, updated).astype(BF)
    accum_out_ref[...] = accum


def cold_update(parts, hits, table, accum, bits):
    return pl.pallas_call(
        cold_update_kernel,
        in_specs=[pl.BlockSpec(memory_space=pltpu.VMEM)] * 5,
        out_specs=[pl.BlockSpec(memory_space=pltpu.VMEM)] * 2,
        out_shape=[
            jax.ShapeDtypeStruct(table.shape, BF),
            jax.ShapeDtypeStruct(accum.shape, F32),
        ],
        compiler_params=pltpu.CompilerParams(vmem_limit_bytes=VMEM_LIMIT),
    )(parts, hits, table, accum, bits)


def swap(block, axis):
    return lax.all_to_all(block, axis, split_axis=0, concat_axis=0, tiled=True)


def on_device(
    cold_table,
    cold_accum,
    dither_bits,
    hot_table,
    hot_accum,
    w_flat,
    w_inter,
    hidden_bias,
    w_out,
    targets,
    hot_ids,
    cold_slots,
    requests,
    counts,
):
    shards = lax.axis_size("shard")
    copies = lax.axis_size("dp")
    micros = counts.shape[0]
    capacity = requests.shape[1]
    row_count, width = cold_table.shape
    hot_count = hot_table.shape[0]
    samples = targets.shape[0] // micros
    feats = cold_slots.shape[1] + hot_ids.shape[1]

    asked = requests.reshape(micros, shards, capacity)
    live = jnp.arange(capacity, dtype=jnp.int32)[None, None, :] < counts[:, :, None]
    asked = jnp.where(live, asked, -1).transpose(1, 0, 2)
    requested = swap(asked.reshape(shards, micros * capacity), "shard")
    requested = requested.reshape(shards, micros, capacity)

    fetched = []
    hits = jnp.zeros((1, row_count), F32)
    for m in range(micros):
        rows, part_hits = owner_gather(requested[:, m].reshape(-1, 1), cold_table)
        hits = hits + part_hits
        fetched.append(
            swap(rows.reshape(shards, capacity, width), "shard").reshape(shards * capacity, width)
        )
    hits = lax.psum(hits.reshape(row_count), "dp")

    turned = w_inter.reshape(feats, feats, -1).transpose(1, 0, 2).reshape(w_inter.shape)
    hot_rows = hot_table.astype(BF)
    cold_ids = cold_slots.reshape(micros, samples, -1).transpose(0, 2, 1).reshape(micros, -1)
    hot_names = hot_ids.reshape(micros, samples, -1).transpose(0, 2, 1).reshape(micros, -1)
    hot_grad = jnp.zeros(hot_table.shape, F32)
    owner_parts = []
    for m in range(micros):
        slot_grad, hot_grad = train(
            fetched[m],
            cold_ids[m].reshape(-1, 1),
            cold_ids[m].reshape(1, -1),
            hot_names[m].reshape(-1, 1),
            hot_names[m].reshape(1, -1),
            hot_rows,
            w_flat,
            w_inter,
            turned,
            hidden_bias.reshape(1, -1),
            w_out.reshape(1, -1),
            targets[m * samples : (m + 1) * samples].reshape(-1, 1),
            hot_grad,
        )
        owner_parts.append(swap(slot_grad.reshape(shards, capacity, width), "shard"))
    owner_grad = jnp.concatenate([part.reshape(-1, width) for part in owner_parts], axis=0)
    owner_ids = requested.transpose(1, 0, 2).reshape(1, -1)
    cold_grad = owner_scatter(owner_ids, owner_grad, row_count)

    share = row_count // copies
    parts = swap(cold_grad.reshape(copies, share, width), "dp")
    first = lax.axis_index("dp") * share
    cold_out, cold_accum_out = cold_update(
        parts,
        lax.dynamic_slice_in_dim(hits, first, share).reshape(-1, 1),
        lax.dynamic_slice_in_dim(cold_table, first, share),
        lax.dynamic_slice_in_dim(cold_accum, first, share).reshape(-1, 1),
        lax.dynamic_slice_in_dim(dither_bits, first, share),
    )
    cold_out = lax.all_gather(cold_out, "dp", tiled=True)
    cold_accum_out = lax.all_gather(cold_accum_out.reshape(-1), "dp", tiled=True)

    hot_part = jnp.sum(swap(hot_grad.reshape(copies, hot_count // copies, width), "dp"), axis=0)
    hot_part = hot_part.reshape(shards, -1, width)
    hot_part = jnp.sum(swap(hot_part, "shard"), axis=0)
    hot_total = lax.all_gather(hot_part, "shard", tiled=True)
    hot_total = lax.all_gather(hot_total, "dp", tiled=True)
    hot_accum_out = hot_accum + jnp.mean(hot_total * hot_total, axis=-1)
    hot_out = hot_table - learn_rate * hot_total / jnp.sqrt(hot_accum_out)[:, None]
    return (cold_out, cold_accum_out, hot_out, hot_accum_out)


def solution(mesh):
    return jax.shard_map(
        on_device,
        mesh=mesh,
        in_specs=(
            P("shard", None),
            P("shard"),
            P("shard", None),
            P(),
            P(),
            P(),
            P(),
            P(),
            P(),
            P(("shard", "dp")),
            P(("shard", "dp"), None),
            P(("shard", "dp"), None),
            P(("shard", "dp"), None),
            P(("shard", "dp"), None),
        ),
        out_specs=(P("shard", None), P("shard"), P(), P()),
        check_vma=False,
    )
```

```python
import functools

import jax
import jax.numpy as jnp
from jax import lax
from jax.experimental import pallas as pl
from jax.experimental.pallas import tpu as pltpu
from jax.sharding import PartitionSpec as P

learn_rate = 0.3
BF = jnp.bfloat16
F32 = jnp.float32
VMEM_LIMIT = 52 * 1024 * 1024


def dot(a, b):
    return lax.dot_general(a, b, (((1,), (0,)), ((), ())), preferred_element_type=F32)


def dot_t(a, b):
    return lax.dot_general(a, b, (((1,), (1,)), ((), ())), preferred_element_type=F32)


def hot_one(rows, columns, ids, axis, first):
    spots = lax.broadcasted_iota(jnp.int32, (rows, columns), axis) + first
    return jnp.where(spots == ids, 1.0, 0.0)


def owner_gather_kernel(ids_ref, table_ref, rows_ref, hits_ref):
    rows = table_ref.shape[0]
    pick = hot_one(ids_ref.shape[0], rows, ids_ref[...], 1, 0)
    rows_ref[...] = dot(pick.astype(BF), table_ref[...]).astype(BF)

    @pl.when(pl.program_id(0) == 0)
    def _():
        hits_ref[...] = jnp.zeros_like(hits_ref)

    hits_ref[...] += jnp.sum(pick, axis=0, keepdims=True)


def owner_gather(ids, table):
    count, (rows, width) = ids.shape[0], table.shape
    tile = min(256, count)
    return pl.pallas_call(
        owner_gather_kernel,
        grid=(count // tile,),
        in_specs=[
            pl.BlockSpec((tile, 1), lambda i: (i, 0)),
            pl.BlockSpec((rows, width), lambda i: (0, 0)),
        ],
        out_specs=[
            pl.BlockSpec((tile, width), lambda i: (i, 0)),
            pl.BlockSpec((1, rows), lambda i: (0, 0)),
        ],
        out_shape=[
            jax.ShapeDtypeStruct((count, width), BF),
            jax.ShapeDtypeStruct((1, rows), F32),
        ],
        compiler_params=pltpu.CompilerParams(vmem_limit_bytes=VMEM_LIMIT),
        cost_estimate=pl.CostEstimate(
            flops=2 * count * rows * width,
            bytes_accessed=2 * (count + rows) * width,
            transcendentals=0,
        ),
    )(ids, table)


def train_kernel(
    fetched_ref,
    cold_col_ref,
    cold_row_ref,
    hot_col_ref,
    hot_row_ref,
    hot_ref,
    w_flat_ref,
    w_inter_ref,
    w_turned_ref,
    bias_ref,
    w_out_ref,
    targets_ref,
    hot_before_ref,
    slot_grad_ref,
    hot_grad_ref,
    x_ref,
    pairs_ref,
    grad_ref,
    high_ref,
    low_ref,
):
    feats, samples, width = x_ref.shape
    cold = cold_col_ref.shape[0] // samples
    slots = fetched_ref.shape[0]
    hot_count = hot_ref.shape[0]
    scale = width ** (-0.5)
    group = 16
    side = feats * group
    square = feats * feats

    def fill_cold(f, carry):
        ids = cold_col_ref[pl.ds(pl.multiple_of(f * samples, samples), samples), :]
        pick = hot_one(samples, slots, ids, 1, 0).astype(BF)
        x_ref[f] = dot(pick, fetched_ref[...]).astype(BF)
        return carry

    lax.fori_loop(0, cold, fill_cold, 0)

    def fill_hot(f, carry):
        ids = hot_col_ref[pl.ds(pl.multiple_of(f * samples, samples), samples), :]
        pick = hot_one(samples, hot_count, ids, 1, 0).astype(BF)
        x_ref[f + cold] = dot(pick, hot_ref[...]).astype(BF)
        return carry

    lax.fori_loop(0, feats - cold, fill_hot, 0)

    def grid_of(shape, axis):
        return lax.broadcasted_iota(jnp.int32, shape, axis)

    same_sample = grid_of((side, side), 0) % group == grid_of((side, side), 1) % group
    same_feature = grid_of((side, square), 0) // group == grid_of((side, square), 1) // feats
    spread = jnp.where(
        grid_of((side, square), 0) // group == grid_of((side, square), 1) % feats, 1.0, 0.0
    ).astype(BF)

    def pair_step(b, carry):
        at = pl.ds(pl.multiple_of(b * group, group), group)
        part = x_ref[:, at, :].reshape(side, width)
        grams = dot_t(part, part) * scale
        grams = jnp.where(same_sample, grams, 0.0).astype(BF)
        wide = jnp.where(same_feature, dot(grams, spread), 0.0)
        pairs_ref[at, :] = jnp.sum(wide.reshape(feats, group, square), axis=0).astype(BF)
        return carry

    lax.fori_loop(0, samples // group, pair_step, 0, unroll=2)

    pre = dot(pairs_ref[...], w_inter_ref[...]) + bias_ref[...]
    for f in range(feats):
        pre = pre + dot(x_ref[f], w_flat_ref[f * width : (f + 1) * width, :])
    gated = jax.nn.sigmoid(pre)
    w_out = w_out_ref[...]
    logits = jnp.sum(pre * gated * w_out, axis=-1, keepdims=True)
    residual = jax.nn.sigmoid(logits) - targets_ref[...]
    slopes = (residual * w_out * gated * (1.0 + pre * (1.0 - gated))).astype(BF)

    mirror = (dot_t(slopes, w_inter_ref[...]) + dot_t(slopes, w_turned_ref[...])) * scale
    pairs_ref[...] = mirror.astype(BF)

    def mirror_step(b, carry):
        at = pl.ds(pl.multiple_of(b * group, group), group)
        part = x_ref[:, at, :].reshape(side, width)
        one = pairs_ref[at, :].astype(F32)
        many = jnp.broadcast_to(one[None], (feats, group, square)).reshape(side, square)
        many = jnp.where(same_feature, many, 0.0).astype(BF)
        turned = jnp.where(same_sample, dot_t(many, spread), 0.0).astype(BF)
        grad_ref[:, at, :] = dot(turned, part).reshape(feats, group, width)
        return carry

    lax.fori_loop(0, samples // group, mirror_step, 0, unroll=2)

    for f in range(feats):
        back = dot_t(slopes, w_flat_ref[f * width : (f + 1) * width, :]) + grad_ref[f]
        high = back.astype(BF)
        high_ref[f * samples : (f + 1) * samples, :] = high
        if f >= cold:
            low_ref[(f - cold) * samples : (f - cold + 1) * samples, :] = (
                back - high.astype(F32)
            ).astype(BF)

    tile = 256
    edge = cold * samples

    def spill_cold(c, carry):
        first = pl.multiple_of(c * tile, tile)
        pick = hot_one(tile, edge, cold_row_ref[...], 0, first).astype(BF)
        slot_grad_ref[pl.ds(first, tile), :] = dot(pick, high_ref[:edge, :]).astype(BF)
        return carry

    lax.fori_loop(0, slots // tile, spill_cold, 0)

    def spill_hot(c, carry):
        first = pl.multiple_of(c * tile, tile)
        pick = hot_one(tile, hot_row_ref.shape[1], hot_row_ref[...], 0, first).astype(BF)
        total = dot(pick, high_ref[edge:, :]) + dot(pick, low_ref[...])
        at = pl.ds(first, tile)
        hot_grad_ref[at, :] = hot_before_ref[at, :] + total
        return carry

    lax.fori_loop(0, hot_count // tile, spill_hot, 0)


def train(*operands):
    fetched, cold_col, _, hot_col, _, hot_rows, w_flat = operands[:7]
    samples = operands[11].shape[0]
    slots, width = fetched.shape
    feats = (cold_col.shape[0] + hot_col.shape[0]) // samples
    hidden = w_flat.shape[1]
    return pl.pallas_call(
        train_kernel,
        in_specs=[pl.BlockSpec(memory_space=pltpu.VMEM)] * len(operands),
        out_specs=[pl.BlockSpec(memory_space=pltpu.VMEM)] * 2,
        out_shape=[
            jax.ShapeDtypeStruct((slots, width), BF),
            jax.ShapeDtypeStruct(hot_rows.shape, F32),
        ],
        scratch_shapes=[
            pltpu.VMEM((feats, samples, width), BF),
            pltpu.VMEM((samples, feats * feats), BF),
            pltpu.VMEM((feats, samples, width), F32),
            pltpu.VMEM((feats * samples, width), BF),
            pltpu.VMEM((hot_col.shape[0], width), BF),
        ],
        compiler_params=pltpu.CompilerParams(vmem_limit_bytes=VMEM_LIMIT),
        cost_estimate=pl.CostEstimate(
            flops=4 * samples * feats * width * (hidden + slots + hot_rows.shape[0]),
            bytes_accessed=12 * 1024 * 1024,
            transcendentals=samples * hidden,
        ),
    )(*operands)


def to_column(row):
    return jnp.transpose(jnp.broadcast_to(row, (8, row.shape[1])))[:, :1]


def to_row(column):
    return jnp.transpose(jnp.broadcast_to(column, (column.shape[0], 128)))[:1, :]


def tail_kernel(
    shards,
    copies,
    micros,
    ids_ref,
    hits_ref,
    table_ref,
    accum_ref,
    bits_ref,
    hot_grad_ref,
    hot_table_ref,
    hot_accum_ref,
    *rest,
):
    slot_refs = rest[:micros]
    cold_out_ref, accum_out_ref, hot_out_ref, hot_accum_out_ref = rest[micros : micros + 4]
    (
        grads_ref,
        parts_ref,
        gathered_ref,
        hits_in_ref,
        dp_in_ref,
        quarter_ref,
        shard_in_ref,
        total_ref,
        cold_send,
        cold_recv,
        hits_send,
        hits_recv,
        dp_send,
        dp_recv,
        shard_send,
        shard_recv,
        spread_send,
        spread_recv,
        wide_send,
        wide_recv,
        part_send,
        part_recv,
        out_send,
        out_recv,
        accum_send,
        accum_recv,
    ) = rest[micros + 4 :]
    s = lax.axis_index("shard")
    d = lax.axis_index("dp")
    share, width = parts_ref.shape[1:]

    def along_shard(k):
        return lax.rem(s + k, shards)

    def along_dp(k):
        return lax.rem(d + k, copies)

    barrier = pltpu.get_barrier_semaphore()
    for k in range(1, shards):
        pl.semaphore_signal(
            barrier, inc=1, device_id=(along_shard(k), d), device_id_type=pl.DeviceIdType.MESH
        )
    for k in range(1, copies):
        pl.semaphore_signal(
            barrier, inc=1, device_id=(s, along_dp(k)), device_id_type=pl.DeviceIdType.MESH
        )
    pl.semaphore_wait(barrier, shards + copies - 2)

    def send(src, dst, send_sem, recv_sem, device):
        copy = pltpu.make_async_remote_copy(
            src_ref=src,
            dst_ref=dst,
            send_sem=send_sem,
            recv_sem=recv_sem,
            device_id=device,
            device_id_type=pl.DeviceIdType.MESH,
        )
        copy.start()
        return copy

    def to_dp(k, src, dst, sends, receives):
        return send(src, dst, sends.at[k - 1], receives.at[k - 1], (s, along_dp(k)))

    def to_shard(k, src, dst, sends, receives, at=0):
        j = at * (shards - 1) + k - 1
        return send(src, dst, sends.at[j], receives.at[j], (along_shard(k), d))

    hot_first = [
        to_dp(k, hot_grad_ref.at[along_dp(k)], dp_in_ref.at[d], dp_send, dp_recv)
        for k in range(1, copies)
    ]
    hit_copies = [
        to_dp(k, hits_ref.at[along_dp(k)], hits_in_ref.at[d], hits_send, hits_recv)
        for k in range(1, copies)
    ]
    cold_copies = [
        to_shard(k, slot_refs[m].at[along_shard(k)], grads_ref.at[m, s], cold_send, cold_recv, m)
        for m in range(micros)
        for k in range(1, shards)
    ]
    for m in range(micros):
        grads_ref[m, s] = slot_refs[m][s]

    for copy in hot_first:
        copy.wait_recv()
    quarter_ref[...] = hot_grad_ref[d]
    for k in range(1, copies):
        quarter_ref[...] += dp_in_ref[along_dp(k)]
    hot_second = [
        to_shard(k, quarter_ref.at[along_shard(k)], shard_in_ref.at[s], shard_send, shard_recv)
        for k in range(1, shards)
    ]
    for copy in hot_second:
        copy.wait_recv()
    total = quarter_ref[s]
    for k in range(1, shards):
        total = total + shard_in_ref[along_shard(k)]
    total_ref[d, s] = total
    hot_third = [
        to_shard(k, total_ref.at[d, s], total_ref.at[d, s], spread_send, spread_recv)
        for k in range(1, shards)
    ]
    for copy in hot_third:
        copy.wait_recv()
    hot_fourth = [
        to_dp(k, total_ref.at[d], total_ref.at[d], wide_send, wide_recv) for k in range(1, copies)
    ]

    for copy in cold_copies:
        copy.wait_recv()
    tile = min(256, share)

    def scatter(q):
        def step(t, carry):
            at = pl.multiple_of(t * tile, tile)
            pick = hot_one(tile, ids_ref.shape[1], ids_ref[...], 0, q * share + at).astype(BF)
            grads = grads_ref[...].reshape(-1, width)
            parts_ref[q, pl.ds(at, tile), :] = dot(pick, grads).astype(BF)
            return carry

        lax.fori_loop(0, share // tile, step, 0)

    part_copies = []
    for k in range(1, copies):
        q = along_dp(k)
        scatter(q)
        part_copies.append(to_dp(k, parts_ref.at[q], gathered_ref.at[d], part_send, part_recv))
    scatter(d)

    for copy in hit_copies + part_copies:
        copy.wait_recv()
    grad = parts_ref[d].astype(F32)
    hits = hits_ref[d]
    for k in range(1, copies):
        grad = grad + gathered_ref[along_dp(k)].astype(F32)
        hits = hits + hits_in_ref[along_dp(k)]
    own = pl.ds(pl.multiple_of(d * share, share), share)
    hits = to_column(hits)
    averaged = grad / jnp.maximum(hits, 1.0)
    accum = to_column(accum_ref[d]) + jnp.mean(averaged * averaged, axis=-1, keepdims=True)
    accum_out_ref[d] = to_row(accum)
    accum_copies = [
        to_dp(k, accum_out_ref.at[d], accum_out_ref.at[d], accum_send, accum_recv)
        for k in range(1, copies)
    ]
    updated = table_ref[own, :].astype(F32) - learn_rate * averaged / jnp.sqrt(accum)
    step = jnp.max(jnp.abs(updated), axis=-1, keepdims=True) / 8.0
    dither = bits_ref[own, :].astype(F32) * (1.0 / 65280.0) - 0.5
    cold_out_ref[d] = jnp.where(hits > 0.5, updated + step * dither, updated).astype(BF)
    out_copies = [
        to_dp(k, cold_out_ref.at[d], cold_out_ref.at[d], out_send, out_recv)
        for k in range(1, copies)
    ]

    for copy in hot_fourth:
        copy.wait_recv()
    hot_sum = total_ref[...].reshape(hot_table_ref.shape)
    hot_accum = to_column(hot_accum_ref[...]) + jnp.mean(hot_sum * hot_sum, axis=-1, keepdims=True)
    hot_out_ref[...] = hot_table_ref[...] - learn_rate * hot_sum / jnp.sqrt(hot_accum)
    hot_accum_out_ref[...] = to_row(hot_accum)

    for copy in accum_copies + out_copies:
        copy.wait_recv()
    for group in (hot_first, hit_copies, cold_copies, hot_second, hot_third, hot_fourth):
        for copy in group:
            copy.wait_send()
    for copy in part_copies + accum_copies + out_copies:
        copy.wait_send()


def tail(ids, hits, table, accum, bits, hot_grad, hot_table, hot_accum, slot_grads):
    shards = lax.axis_size("shard")
    copies = lax.axis_size("dp")
    micros = len(slot_grads)
    rows, width = table.shape
    share = rows // copies
    hot_count = hot_table.shape[0]
    piece = hot_count // (shards * copies)
    capacity = slot_grads[0].shape[1]
    operands = (
        ids,
        hits.reshape(copies, 1, share),
        table,
        accum.reshape(copies, 1, share),
        bits,
        hot_grad.reshape(copies, shards, piece, width),
        hot_table,
        hot_accum.reshape(1, -1),
        *slot_grads,
    )
    shard_sem = pltpu.SemaphoreType.DMA((shards - 1,))
    cold_sem = pltpu.SemaphoreType.DMA((micros * (shards - 1),))
    dp_sem = pltpu.SemaphoreType.DMA((copies - 1,))
    outs = pl.pallas_call(
        functools.partial(tail_kernel, shards, copies, micros),
        in_specs=[pl.BlockSpec(memory_space=pltpu.VMEM)] * len(operands),
        out_specs=[pl.BlockSpec(memory_space=pltpu.VMEM)] * 4,
        out_shape=[
            jax.ShapeDtypeStruct((copies, share, width), BF),
            jax.ShapeDtypeStruct((copies, 1, share), F32),
            jax.ShapeDtypeStruct(hot_table.shape, F32),
            jax.ShapeDtypeStruct((1, hot_count), F32),
        ],
        scratch_shapes=[
            pltpu.VMEM((micros, shards, capacity, width), BF),
            pltpu.VMEM((copies, share, width), BF),
            pltpu.VMEM((copies, share, width), BF),
            pltpu.VMEM((copies, 1, share), F32),
            pltpu.VMEM((copies, shards, piece, width), F32),
            pltpu.VMEM((shards, piece, width), F32),
            pltpu.VMEM((shards, piece, width), F32),
            pltpu.VMEM((copies, shards, piece, width), F32),
            cold_sem,
            cold_sem,
            dp_sem,
            dp_sem,
            dp_sem,
            dp_sem,
            shard_sem,
            shard_sem,
            shard_sem,
            shard_sem,
            dp_sem,
            dp_sem,
            dp_sem,
            dp_sem,
            dp_sem,
            dp_sem,
            dp_sem,
            dp_sem,
        ],
        compiler_params=pltpu.CompilerParams(
            vmem_limit_bytes=VMEM_LIMIT, collective_id=1, has_side_effects=True
        ),
    )(*operands)
    cold_out, accum_out, hot_out, hot_accum_out = outs
    return (
        cold_out.reshape(rows, width),
        accum_out.reshape(rows),
        hot_out,
        hot_accum_out.reshape(hot_count),
    )


def swap(block, axis):
    return lax.all_to_all(block, axis, split_axis=0, concat_axis=0, tiled=True)


def on_device(
    cold_table,
    cold_accum,
    dither_bits,
    hot_table,
    hot_accum,
    w_flat,
    w_inter,
    hidden_bias,
    w_out,
    targets,
    hot_ids,
    cold_slots,
    requests,
    counts,
):
    shards = lax.axis_size("shard")
    micros = counts.shape[0]
    capacity = requests.shape[1]
    row_count, width = cold_table.shape
    samples = targets.shape[0] // micros
    feats = cold_slots.shape[1] + hot_ids.shape[1]

    asked = requests.reshape(micros, shards, capacity)
    live = jnp.arange(capacity, dtype=jnp.int32)[None, None, :] < counts[:, :, None]
    asked = jnp.where(live, asked, -1).transpose(1, 0, 2)
    requested = swap(asked.reshape(shards, micros * capacity), "shard")
    requested = requested.reshape(shards, micros, capacity)

    fetched = []
    hits = jnp.zeros((1, row_count), F32)
    for m in range(micros):
        rows, part_hits = owner_gather(requested[:, m].reshape(-1, 1), cold_table)
        hits = hits + part_hits
        fetched.append(
            swap(rows.reshape(shards, capacity, width), "shard").reshape(shards * capacity, width)
        )

    turned = w_inter.reshape(feats, feats, -1).transpose(1, 0, 2).reshape(w_inter.shape)
    hot_rows = hot_table.astype(BF)
    cold_ids = cold_slots.reshape(micros, samples, -1).transpose(0, 2, 1).reshape(micros, -1)
    hot_names = hot_ids.reshape(micros, samples, -1).transpose(0, 2, 1).reshape(micros, -1)
    hot_grad = jnp.zeros(hot_table.shape, F32)
    slot_grads = []
    for m in range(micros):
        slot_grad, hot_grad = train(
            fetched[m],
            cold_ids[m].reshape(-1, 1),
            cold_ids[m].reshape(1, -1),
            hot_names[m].reshape(-1, 1),
            hot_names[m].reshape(1, -1),
            hot_rows,
            w_flat,
            w_inter,
            turned,
            hidden_bias.reshape(1, -1),
            w_out.reshape(1, -1),
            targets[m * samples : (m + 1) * samples].reshape(-1, 1),
            hot_grad,
        )
        slot_grads.append(slot_grad.reshape(shards, capacity, width))
    owner_ids = requested.transpose(1, 0, 2).reshape(1, -1)
    return tail(
        owner_ids,
        hits,
        cold_table,
        cold_accum,
        dither_bits,
        hot_grad,
        hot_table,
        hot_accum,
        slot_grads,
    )


def solution(mesh):
    return jax.shard_map(
        on_device,
        mesh=mesh,
        in_specs=(
            P("shard", None),
            P("shard"),
            P("shard", None),
            P(),
            P(),
            P(),
            P(),
            P(),
            P(),
            P(("shard", "dp")),
            P(("shard", "dp"), None),
            P(("shard", "dp"), None),
            P(("shard", "dp"), None),
            P(("shard", "dp"), None),
        ),
        out_specs=(P("shard", None), P("shard"), P(), P()),
        check_vma=False,
    )
```

```python
import functools

import jax
import jax.numpy as jnp
from jax import lax
from jax.experimental import pallas as pl
from jax.experimental.pallas import tpu as pltpu
from jax.sharding import PartitionSpec as P

learn_rate = 0.3
BF = jnp.bfloat16
F32 = jnp.float32
VMEM_LIMIT = 52 * 1024 * 1024


def dot(a, b):
    return lax.dot_general(a, b, (((1,), (0,)), ((), ())), preferred_element_type=F32)


def dot_t(a, b):
    return lax.dot_general(a, b, (((1,), (1,)), ((), ())), preferred_element_type=F32)


def hot_one(rows, columns, ids, axis, first):
    spots = lax.broadcasted_iota(jnp.int32, (rows, columns), axis) + first
    return jnp.where(spots == ids, 1.0, 0.0)


def train_kernel(
    fetched_ref,
    cold_col_ref,
    cold_row_ref,
    hot_col_ref,
    hot_row_ref,
    hot_ref,
    w_flat_ref,
    w_inter_ref,
    w_turned_ref,
    bias_ref,
    w_out_ref,
    targets_ref,
    hot_before_ref,
    slot_grad_ref,
    hot_grad_ref,
    x_ref,
    pairs_ref,
    grad_ref,
    high_ref,
    low_ref,
):
    feats, samples, width = x_ref.shape
    cold = cold_col_ref.shape[0] // samples
    shards, capacity = fetched_ref.shape[:2]
    slots = shards * capacity
    hot_count = hot_ref.shape[0]
    scale = width ** (-0.5)
    group = 16
    side = feats * group
    square = feats * feats

    def fill_cold(f, carry):
        ids = cold_col_ref[pl.ds(pl.multiple_of(f * samples, samples), samples), :]
        pick = hot_one(samples, slots, ids, 1, 0).astype(BF)
        x_ref[f] = dot(pick, fetched_ref[...].reshape(slots, width)).astype(BF)
        return carry

    lax.fori_loop(0, cold, fill_cold, 0)

    def fill_hot(f, carry):
        ids = hot_col_ref[pl.ds(pl.multiple_of(f * samples, samples), samples), :]
        pick = hot_one(samples, hot_count, ids, 1, 0).astype(BF)
        x_ref[f + cold] = dot(pick, hot_ref[...]).astype(BF)
        return carry

    lax.fori_loop(0, feats - cold, fill_hot, 0)

    def grid_of(shape, axis):
        return lax.broadcasted_iota(jnp.int32, shape, axis)

    same_sample = grid_of((side, side), 0) % group == grid_of((side, side), 1) % group
    same_feature = grid_of((side, square), 0) // group == grid_of((side, square), 1) // feats
    spread = jnp.where(
        grid_of((side, square), 0) // group == grid_of((side, square), 1) % feats, 1.0, 0.0
    ).astype(BF)

    def pair_step(b, carry):
        at = pl.ds(pl.multiple_of(b * group, group), group)
        part = x_ref[:, at, :].reshape(side, width)
        grams = dot_t(part, part) * scale
        grams = jnp.where(same_sample, grams, 0.0).astype(BF)
        wide = jnp.where(same_feature, dot(grams, spread), 0.0)
        pairs_ref[at, :] = jnp.sum(wide.reshape(feats, group, square), axis=0).astype(BF)
        return carry

    lax.fori_loop(0, samples // group, pair_step, 0, unroll=2)

    pre = dot(pairs_ref[...], w_inter_ref[...]) + bias_ref[...]
    for f in range(feats):
        pre = pre + dot(x_ref[f], w_flat_ref[f * width : (f + 1) * width, :])
    gated = jax.nn.sigmoid(pre)
    w_out = w_out_ref[...]
    logits = jnp.sum(pre * gated * w_out, axis=-1, keepdims=True)
    residual = jax.nn.sigmoid(logits) - targets_ref[...]
    slopes = (residual * w_out * gated * (1.0 + pre * (1.0 - gated))).astype(BF)

    mirror = (dot_t(slopes, w_inter_ref[...]) + dot_t(slopes, w_turned_ref[...])) * scale
    pairs_ref[...] = mirror.astype(BF)

    def mirror_step(b, carry):
        at = pl.ds(pl.multiple_of(b * group, group), group)
        part = x_ref[:, at, :].reshape(side, width)
        one = pairs_ref[at, :].astype(F32)
        many = jnp.broadcast_to(one[None], (feats, group, square)).reshape(side, square)
        many = jnp.where(same_feature, many, 0.0).astype(BF)
        turned = jnp.where(same_sample, dot_t(many, spread), 0.0).astype(BF)
        grad_ref[:, at, :] = dot(turned, part).reshape(feats, group, width)
        return carry

    lax.fori_loop(0, samples // group, mirror_step, 0, unroll=2)

    for f in range(feats):
        back = dot_t(slopes, w_flat_ref[f * width : (f + 1) * width, :]) + grad_ref[f]
        high = back.astype(BF)
        high_ref[f * samples : (f + 1) * samples, :] = high
        if f >= cold:
            low_ref[(f - cold) * samples : (f - cold + 1) * samples, :] = (
                back - high.astype(F32)
            ).astype(BF)

    edge = cold * samples
    tile = max(256, capacity)
    owners = tile // capacity

    def spill_cold(c, carry):
        pick = hot_one(tile, edge, cold_row_ref[...], 0, c * tile).astype(BF)
        summed = dot(pick, high_ref[:edge, :]).astype(BF)
        slot_grad_ref[pl.ds(c * owners, owners)] = summed.reshape(owners, capacity, width)
        return carry

    lax.fori_loop(0, slots // tile, spill_cold, 0)
    tile = min(256, hot_count)

    def spill_hot(c, carry):
        first = pl.multiple_of(c * tile, tile)
        pick = hot_one(tile, hot_row_ref.shape[1], hot_row_ref[...], 0, first).astype(BF)
        total = dot(pick, high_ref[edge:, :]) + dot(pick, low_ref[...])
        at = pl.ds(first, tile)
        hot_grad_ref[at, :] = total if hot_before_ref is None else hot_before_ref[at, :] + total
        return carry

    lax.fori_loop(0, hot_count // tile, spill_hot, 0)


def to_column(row):
    return jnp.transpose(jnp.broadcast_to(row, (8, row.shape[1])))[:, :1]


def to_row(column):
    return jnp.transpose(jnp.broadcast_to(column, (column.shape[0], 128)))[:1, :]


def train_scratch(feats, samples, width, hot_lookups):
    return [
        pltpu.VMEM((feats, samples, width), BF),
        pltpu.VMEM((samples, feats * feats), BF),
        pltpu.VMEM((feats, samples, width), F32),
        pltpu.VMEM((feats * samples, width), BF),
        pltpu.VMEM((hot_lookups, width), BF),
    ]


def send(src, dst, send_sem, recv_sem, device):
    copy = pltpu.make_async_remote_copy(
        src_ref=src,
        dst_ref=dst,
        send_sem=send_sem,
        recv_sem=recv_sem,
        device_id=device,
        device_id_type=pl.DeviceIdType.MESH,
    )
    copy.start()
    return copy


def fetch_kernel(shards, micros, asked_ref, table_ref, *rest):
    network = rest[:11]
    fetched_ref, requested_ref, hits_ref, slot_grad_ref, hot_grad_ref = rest[11:16]
    rows_ref = rest[16]
    scratch = rest[17:22]
    ask_send, ask_recv, row_send, row_recv = rest[22:]
    s = lax.axis_index("shard")
    d = lax.axis_index("dp")
    capacity = fetched_ref.shape[2]
    rows = table_ref.shape[0]

    def along_shard(k):
        return lax.rem(s + k, shards)

    barrier = pltpu.get_barrier_semaphore()
    for k in range(1, shards):
        pl.semaphore_signal(
            barrier, inc=1, device_id=(along_shard(k), d), device_id_type=pl.DeviceIdType.MESH
        )
    pl.semaphore_wait(barrier, shards - 1)

    asks = []
    for k in range(1, shards):
        p = along_shard(k)
        sems = (ask_send.at[k - 1], ask_recv.at[k - 1])
        asks.append(send(asked_ref.at[p], requested_ref.at[s], *sems, (p, d)))
    requested_ref[s] = asked_ref[s]
    for copy in asks:
        copy.wait_recv()

    hits_ref[...] = jnp.zeros_like(hits_ref)
    moves = []
    for m in range(micros):
        sent = []
        for k in [*range(1, shards), 0]:
            p = along_shard(k)
            ids = to_column(requested_ref[p])[m * capacity : (m + 1) * capacity, :]
            pick = hot_one(capacity, rows, ids, 1, 0)
            hits_ref[...] += jnp.sum(pick, axis=0, keepdims=True)
            found = dot(pick.astype(BF), table_ref[...]).astype(BF)
            if k == 0:
                fetched_ref[m, s] = found
                continue
            rows_ref[m, p] = found
            j = m * (shards - 1) + k - 1
            sems = (row_send.at[j], row_recv.at[j])
            sent.append(send(rows_ref.at[m, p], fetched_ref.at[m, s], *sems, (p, d)))
        moves.append(sent)

    for copy in moves[0]:
        copy.wait_recv()
    train_kernel(fetched_ref.at[0], *network, None, slot_grad_ref, hot_grad_ref, *scratch)
    for sent in moves[1:]:
        for copy in sent:
            copy.wait_recv()
    for copy in asks + sum(moves, []):
        copy.wait_send()


def fetch(asked, table, network, micros):
    shards, _, asked_count = asked.shape
    capacity = asked_count // micros
    rows, width = table.shape
    hot_rows = network[4]
    samples = network[-1].shape[0]
    cold_lookups, hot_lookups = network[0].shape[0], network[2].shape[0]
    feats = (cold_lookups + hot_lookups) // samples
    operands = (asked, table, *network)
    ask_sem = pltpu.SemaphoreType.DMA((shards - 1,))
    row_sem = pltpu.SemaphoreType.DMA((micros * (shards - 1),))
    return pl.pallas_call(
        functools.partial(fetch_kernel, shards, micros),
        in_specs=[pl.BlockSpec(memory_space=pltpu.VMEM)] * len(operands),
        out_specs=[pl.BlockSpec(memory_space=pltpu.VMEM)] * 5,
        out_shape=[
            jax.ShapeDtypeStruct((micros, shards, capacity, width), BF),
            jax.ShapeDtypeStruct(asked.shape, jnp.int32),
            jax.ShapeDtypeStruct((1, rows), F32),
            jax.ShapeDtypeStruct((shards, capacity, width), BF),
            jax.ShapeDtypeStruct(hot_rows.shape, F32),
        ],
        scratch_shapes=[
            pltpu.VMEM((micros, shards, capacity, width), BF),
            *train_scratch(feats, samples, width, hot_lookups),
            ask_sem,
            ask_sem,
            row_sem,
            row_sem,
        ],
        compiler_params=pltpu.CompilerParams(
            vmem_limit_bytes=VMEM_LIMIT, collective_id=0, has_side_effects=True
        ),
    )(*operands)


def tail_kernel(
    shards,
    copies,
    micros,
    ids_ref,
    hits_ref,
    table_ref,
    accum_ref,
    bits_ref,
    hot_before_ref,
    hot_table_ref,
    hot_accum_ref,
    slot_before_ref,
    fetched_ref,
    *rest,
):
    networks = [rest[i * 11 : i * 11 + 11] for i in range(micros - 1)]
    rest = rest[11 * (micros - 1) :]
    cold_out_ref, accum_out_ref, hot_out_ref, hot_accum_out_ref = rest[:4]
    slots_ref, hot_grad_ref = rest[4:6]
    scratch = rest[6:11]
    (
        grads_ref,
        parts_ref,
        gathered_ref,
        hits_in_ref,
        dp_in_ref,
        quarter_ref,
        shard_in_ref,
        total_ref,
        cold_send,
        cold_recv,
        hits_send,
        hits_recv,
        dp_send,
        dp_recv,
        shard_send,
        shard_recv,
        spread_send,
        spread_recv,
        wide_send,
        wide_recv,
        part_send,
        part_recv,
        out_send,
        out_recv,
        accum_send,
        accum_recv,
    ) = rest[11:]
    s = lax.axis_index("shard")
    d = lax.axis_index("dp")
    share, width = parts_ref.shape[1:]
    quarter = dp_in_ref.shape[1]

    def along_shard(k):
        return lax.rem(s + k, shards)

    def along_dp(k):
        return lax.rem(d + k, copies)

    barrier = pltpu.get_barrier_semaphore()
    for k in range(1, shards):
        pl.semaphore_signal(
            barrier, inc=1, device_id=(along_shard(k), d), device_id_type=pl.DeviceIdType.MESH
        )
    for k in range(1, copies):
        pl.semaphore_signal(
            barrier, inc=1, device_id=(s, along_dp(k)), device_id_type=pl.DeviceIdType.MESH
        )
    pl.semaphore_wait(barrier, shards + copies - 2)

    def to_dp(k, src, dst, sends, receives):
        return send(src, dst, sends.at[k - 1], receives.at[k - 1], (s, along_dp(k)))

    def to_shard(k, src, dst, sends, receives, at=0):
        j = at * (shards - 1) + k - 1
        return send(src, dst, sends.at[j], receives.at[j], (along_shard(k), d))

    hit_copies = [
        to_dp(k, hits_ref.at[along_dp(k)], hits_in_ref.at[d], hits_send, hits_recv)
        for k in range(1, copies)
    ]
    cold_copies = [
        to_shard(k, slot_before_ref.at[along_shard(k)], grads_ref.at[0, s], cold_send, cold_recv)
        for k in range(1, shards)
    ]
    grads_ref[0, s] = slot_before_ref[s]
    before = hot_before_ref
    for m in range(1, micros):
        made_ref = slots_ref.at[m - 1]
        train_kernel(
            fetched_ref.at[m], *networks[m - 1], before, made_ref, hot_grad_ref, *scratch
        )
        before = hot_grad_ref
        if m == micros - 1:
            hot_first = [
                to_dp(
                    k,
                    hot_grad_ref.at[pl.ds(pl.multiple_of(along_dp(k) * quarter, 8), quarter)],
                    dp_in_ref.at[d],
                    dp_send,
                    dp_recv,
                )
                for k in range(1, copies)
            ]
        cold_copies += [
            to_shard(k, made_ref.at[along_shard(k)], grads_ref.at[m, s], cold_send, cold_recv, m)
            for k in range(1, shards)
        ]
        grads_ref[m, s] = made_ref[s]

    for copy in hot_first:
        copy.wait_recv()
    summed = hot_grad_ref[pl.ds(pl.multiple_of(d * quarter, 8), quarter), :]
    for k in range(1, copies):
        summed = summed + dp_in_ref[along_dp(k)]
    quarter_ref[...] = summed.reshape(quarter_ref.shape)
    hot_second = [
        to_shard(k, quarter_ref.at[along_shard(k)], shard_in_ref.at[s], shard_send, shard_recv)
        for k in range(1, shards)
    ]
    for copy in hot_second:
        copy.wait_recv()
    total = quarter_ref[s]
    for k in range(1, shards):
        total = total + shard_in_ref[along_shard(k)]
    total_ref[d, s] = total
    hot_third = [
        to_shard(k, total_ref.at[d, s], total_ref.at[d, s], spread_send, spread_recv)
        for k in range(1, shards)
    ]
    for copy in hot_third:
        copy.wait_recv()
    hot_fourth = [
        to_dp(k, total_ref.at[d], total_ref.at[d], wide_send, wide_recv) for k in range(1, copies)
    ]

    for copy in cold_copies:
        copy.wait_recv()
    tile = min(256, share)

    def scatter(q):
        def step(t, carry):
            at = pl.multiple_of(t * tile, tile)
            pick = hot_one(tile, ids_ref.shape[1], ids_ref[...], 0, q * share + at).astype(BF)
            grads = grads_ref[...].reshape(-1, width)
            parts_ref[q, pl.ds(at, tile), :] = dot(pick, grads).astype(BF)
            return carry

        lax.fori_loop(0, share // tile, step, 0)

    part_copies = []
    for k in range(1, copies):
        q = along_dp(k)
        scatter(q)
        part_copies.append(to_dp(k, parts_ref.at[q], gathered_ref.at[d], part_send, part_recv))
    scatter(d)

    for copy in hit_copies + part_copies:
        copy.wait_recv()
    grad = parts_ref[d].astype(F32)
    hits = hits_ref[d]
    for k in range(1, copies):
        grad = grad + gathered_ref[along_dp(k)].astype(F32)
        hits = hits + hits_in_ref[along_dp(k)]
    own = pl.ds(pl.multiple_of(d * share, share), share)
    hits = to_column(hits)
    averaged = grad / jnp.maximum(hits, 1.0)
    accum = to_column(accum_ref[d]) + jnp.mean(averaged * averaged, axis=-1, keepdims=True)
    accum_out_ref[d] = to_row(accum)
    accum_copies = [
        to_dp(k, accum_out_ref.at[d], accum_out_ref.at[d], accum_send, accum_recv)
        for k in range(1, copies)
    ]
    updated = table_ref[own, :].astype(F32) - learn_rate * averaged / jnp.sqrt(accum)
    step = jnp.max(jnp.abs(updated), axis=-1, keepdims=True) / 8.0
    dither = bits_ref[own, :].astype(F32) * (1.0 / 65280.0) - 0.5
    cold_out_ref[d] = jnp.where(hits > 0.5, updated + step * dither, updated).astype(BF)
    out_copies = [
        to_dp(k, cold_out_ref.at[d], cold_out_ref.at[d], out_send, out_recv)
        for k in range(1, copies)
    ]

    for copy in hot_fourth:
        copy.wait_recv()
    hot_sum = total_ref[...].reshape(hot_table_ref.shape)
    hot_accum = to_column(hot_accum_ref[...]) + jnp.mean(hot_sum * hot_sum, axis=-1, keepdims=True)
    hot_out_ref[...] = hot_table_ref[...] - learn_rate * hot_sum / jnp.sqrt(hot_accum)
    hot_accum_out_ref[...] = to_row(hot_accum)

    for copy in accum_copies + out_copies:
        copy.wait_recv()
    for group in (hot_first, hit_copies, cold_copies, hot_second, hot_third, hot_fourth):
        for copy in group:
            copy.wait_send()
    for copy in part_copies + accum_copies + out_copies:
        copy.wait_send()


def tail(
    ids, hits, table, accum, bits, hot_grad, hot_table, hot_accum, slot_grad, fetched, networks
):
    shards = lax.axis_size("shard")
    copies = lax.axis_size("dp")
    micros = fetched.shape[0]
    samples = networks[0][-1].shape[0]
    hot_lookups = networks[0][2].shape[0]
    feats = (networks[0][0].shape[0] + hot_lookups) // samples
    rows, width = table.shape
    share = rows // copies
    hot_count = hot_table.shape[0]
    piece = hot_count // (shards * copies)
    capacity = slot_grad.shape[1]
    operands = (
        ids,
        hits.reshape(copies, 1, share),
        table,
        accum.reshape(copies, 1, share),
        bits,
        hot_grad,
        hot_table,
        hot_accum.reshape(1, -1),
        slot_grad,
        fetched,
        *sum(networks, ()),
    )
    shard_sem = pltpu.SemaphoreType.DMA((shards - 1,))
    cold_sem = pltpu.SemaphoreType.DMA((micros * (shards - 1),))
    dp_sem = pltpu.SemaphoreType.DMA((copies - 1,))
    outs = pl.pallas_call(
        functools.partial(tail_kernel, shards, copies, micros),
        in_specs=[pl.BlockSpec(memory_space=pltpu.VMEM)] * len(operands),
        out_specs=[pl.BlockSpec(memory_space=pltpu.VMEM)] * 4,
        out_shape=[
            jax.ShapeDtypeStruct((copies, share, width), BF),
            jax.ShapeDtypeStruct((copies, 1, share), F32),
            jax.ShapeDtypeStruct(hot_table.shape, F32),
            jax.ShapeDtypeStruct((1, hot_count), F32),
        ],
        scratch_shapes=[
            pltpu.VMEM((micros - 1, shards, capacity, width), BF),
            pltpu.VMEM(hot_table.shape, F32),
            *train_scratch(feats, samples, width, hot_lookups),
            pltpu.VMEM((micros, shards, capacity, width), BF),
            pltpu.VMEM((copies, share, width), BF),
            pltpu.VMEM((copies, share, width), BF),
            pltpu.VMEM((copies, 1, share), F32),
            pltpu.VMEM((copies, shards * piece, width), F32),
            pltpu.VMEM((shards, piece, width), F32),
            pltpu.VMEM((shards, piece, width), F32),
            pltpu.VMEM((copies, shards, piece, width), F32),
            cold_sem,
            cold_sem,
            dp_sem,
            dp_sem,
            dp_sem,
            dp_sem,
            shard_sem,
            shard_sem,
            shard_sem,
            shard_sem,
            dp_sem,
            dp_sem,
            dp_sem,
            dp_sem,
            dp_sem,
            dp_sem,
            dp_sem,
            dp_sem,
        ],
        compiler_params=pltpu.CompilerParams(
            vmem_limit_bytes=VMEM_LIMIT, collective_id=1, has_side_effects=True
        ),
    )(*operands)
    cold_out, accum_out, hot_out, hot_accum_out = outs
    return (
        cold_out.reshape(rows, width),
        accum_out.reshape(rows),
        hot_out,
        hot_accum_out.reshape(hot_count),
    )


def on_device(
    cold_table,
    cold_accum,
    dither_bits,
    hot_table,
    hot_accum,
    w_flat,
    w_inter,
    hidden_bias,
    w_out,
    targets,
    hot_ids,
    cold_slots,
    requests,
    counts,
):
    shards = lax.axis_size("shard")
    micros = counts.shape[0]
    capacity = requests.shape[1]
    samples = targets.shape[0] // micros
    feats = cold_slots.shape[1] + hot_ids.shape[1]

    asked = requests.reshape(micros, shards, capacity)
    live = jnp.arange(capacity, dtype=jnp.int32)[None, None, :] < counts[:, :, None]
    asked = jnp.where(live, asked, -1).transpose(1, 0, 2)
    turned = w_inter.reshape(feats, feats, -1).transpose(1, 0, 2).reshape(w_inter.shape)
    hot_rows = hot_table.astype(BF)
    cold_ids = cold_slots.reshape(micros, samples, -1).transpose(0, 2, 1).reshape(micros, -1)
    hot_names = hot_ids.reshape(micros, samples, -1).transpose(0, 2, 1).reshape(micros, -1)
    networks = [
        (
            cold_ids[m].reshape(-1, 1),
            cold_ids[m].reshape(1, -1),
            hot_names[m].reshape(-1, 1),
            hot_names[m].reshape(1, -1),
            hot_rows,
            w_flat,
            w_inter,
            turned,
            hidden_bias.reshape(1, -1),
            w_out.reshape(1, -1),
            targets[m * samples : (m + 1) * samples].reshape(-1, 1),
        )
        for m in range(micros)
    ]
    fetched, requested, hits, slot_grad, hot_grad = fetch(
        asked.reshape(shards, 1, -1), cold_table, networks[0], micros
    )
    owner_ids = requested.reshape(shards, micros, capacity).transpose(1, 0, 2).reshape(1, -1)
    return tail(
        owner_ids,
        hits,
        cold_table,
        cold_accum,
        dither_bits,
        hot_grad,
        hot_table,
        hot_accum,
        slot_grad,
        fetched,
        networks[1:],
    )


def solution(mesh):
    return jax.shard_map(
        on_device,
        mesh=mesh,
        in_specs=(
            P("shard", None),
            P("shard"),
            P("shard", None),
            P(),
            P(),
            P(),
            P(),
            P(),
            P(),
            P(("shard", "dp")),
            P(("shard", "dp"), None),
            P(("shard", "dp"), None),
            P(("shard", "dp"), None),
            P(("shard", "dp"), None),
        ),
        out_specs=(P("shard", None), P("shard"), P(), P()),
        check_vma=False,
    )
```
